32 devices in a mesh: wide: 8 (over y, x, core), rep: 4 (over z).
Axes of the slice: x: 2, y: 2, z: 4, core: 2. Of those that a mesh axis runs over, the one named last changes fastest.
Arguments:
- record: bfloat16 [32, 256, 8192], P(('wide', 'rep')), may hold values from -90 to 90
- valid: int32 [32, 8192], P(('wide', 'rep')), may hold values 0 or 1
- sources: int32 [3], replicated, may hold values from 0 to 127
Outputs:
- stacks: float32 [128, 192, 8192], P('rep', None, 'wide')
The draws below stay inside these ranges and needn't reach their ends.
Inputs may be any that keep to these rules, and one draw needn't show every extreme that they name: `sources`: block b holds the channels 64 * b to 64 * b + 63.
All inputs are finite; a program needn't handle non-finite values. No bound on the sum of `valid` on one device may be relied on, other than what follows from the above.
Results may differ from the reference program's by a relative error of at most 0.0014.
Values may be sent and summed in bfloat16 or wider, within the bound.
A program may use at most 320 MiB of HBM per device.

```python
import math
import jax
import jax.numpy as jnp
from jax import lax

CH = 8192
WLEN = 256
SRC = 64
NBLK = 3
NSRC = 192
LAGS = 128
HALF_SMOOTH = 5
WINDOWS = 32


def draw_record(key, part):
    keys = jax.random.split(key, 6)
    shape = (WINDOWS, WLEN, CH)
    base = jnp.clip(jax.random.normal(keys[0], shape, jnp.float32), -4.0, 4.0)
    channel_scale = jnp.exp(jax.random.uniform(keys[1], (1, 1, CH), jnp.float32, 0.0, math.log(10.0)))
    window_scale = jax.random.uniform(keys[2], (WINDOWS, 1, CH), jnp.float32, 0.5, 2.0)
    frequency = jax.random.uniform(keys[3], (), jnp.float32, 0.03, 0.2)
    window_phase = jax.random.uniform(keys[4], (WINDOWS, 1, 1), jnp.float32, -math.pi, math.pi)
    channel_phase = jax.random.uniform(keys[5], (1, 1, CH), jnp.float32, -0.5, 0.5)
    times = jnp.arange(WLEN, dtype=jnp.int32).astype(jnp.float32)[None, :, None]
    tone = 0.5 * jnp.sin(2.0 * math.pi * frequency * times + window_phase + channel_phase)
    return ((base + tone) * window_scale * channel_scale).astype(jnp.bfloat16)


def plant(entries, own_key, low, high):
    index_at = [jax.random.randint(jax.random.fold_in(own_key, axis), (), 0, length) for axis, length in enumerate(entries.shape)]
    widest = entries.shape.index(max(entries.shape))
    beside = index_at[:widest] + [(index_at[widest] + 1) % entries.shape[widest]] + index_at[widest + 1:]
    return entries.at[tuple(index_at)].set(low).at[tuple(beside)].set(high)


def setup_inputs(seed: int = 0) -> dict:
    seeds = jax.random.split(jax.random.key(seed), 4)
    return {
        "record": draw_record(jax.random.fold_in(seeds[3], 71), 0),
        "valid": plant((jax.random.randint(seeds[1], (WINDOWS, CH), 0, 8) < 7).astype(jnp.int32), jax.random.fold_in(seeds[1], 1), 0, 1),
        "sources": jax.random.randint(seeds[2], (NBLK,), 0, CH // SRC).astype(jnp.int32),
    }


EPSILON = 1e-05
LEVEL_SHARE = 0.2

def hann_window(length):
    times = jnp.arange(length, dtype=jnp.int32).astype(jnp.float32)
    return 0.5 - 0.5 * jnp.cos(2.0 * math.pi / length * times)

def forward_table(length, bins):
    times = jnp.arange(length, dtype=jnp.int32)[:, None]
    freqs = jnp.arange(1, bins + 1, dtype=jnp.int32)[None, :]
    phase = 2.0 * math.pi / length * jnp.mod(times * freqs, length).astype(jnp.float32)
    return jnp.concatenate([jnp.cos(phase), -jnp.sin(phase)], axis=1).astype(jnp.bfloat16)

def inverse_table(length, bins, lags):
    freqs = jnp.arange(1, bins + 1, dtype=jnp.int32)[:, None]
    shifts = jnp.arange(lags, dtype=jnp.int32)[None, :] - lags // 2
    phase = 2.0 * math.pi / length * jnp.mod(freqs * shifts, length).astype(jnp.float32)
    return jnp.stack([jnp.cos(phase), -jnp.sin(phase)])

def band_matrix(bins):
    rows = jnp.arange(bins, dtype=jnp.int32)[:, None]
    cols = jnp.arange(bins, dtype=jnp.int32)[None, :]
    near = (jnp.abs(rows - cols) <= HALF_SMOOTH).astype(jnp.float32)
    return near / lax.optimization_barrier(jnp.sum(near, axis=1, keepdims=True))

def transform(samples, flags):
    length = samples.shape[1]
    bins = length // 2
    wide_data = samples.astype(jnp.float32)
    centered = wide_data - lax.optimization_barrier(jnp.mean(wide_data, axis=1, keepdims=True))
    tapered = (centered * hann_window(length)[None, :, None]).astype(jnp.bfloat16)
    spectrum = jnp.einsum('wtc,tg->wgc', tapered.astype(jnp.float32), forward_table(length, bins).astype(jnp.float32), precision=lax.Precision.HIGHEST)
    spectrum = spectrum.reshape(spectrum.shape[0], 2, bins, spectrum.shape[2])
    magnitude = jnp.sqrt(spectrum[:, 0] * spectrum[:, 0] + spectrum[:, 1] * spectrum[:, 1])
    smooth = jnp.einsum('fg,wgc->wfc', band_matrix(bins), magnitude, precision=lax.Precision.HIGHEST)
    level = lax.optimization_barrier(jnp.mean(magnitude, axis=1, keepdims=True))
    scaled = spectrum / (smooth + LEVEL_SHARE * level + EPSILON)[:, None]
    scaled = scaled * flags.astype(jnp.float32)[:, None, None, :]
    return scaled.astype(jnp.bfloat16)

def cross_terms(source, receiver):
    source_f = source.astype(jnp.float32)
    receiver_f = receiver.astype(jnp.float32)
    high = lax.Precision.HIGHEST
    real_real = jnp.einsum('wfs,wfc->fsc', source_f[:, 0], receiver_f[:, 0], precision=high)
    imag_imag = jnp.einsum('wfs,wfc->fsc', source_f[:, 1], receiver_f[:, 1], precision=high)
    real_imag = jnp.einsum('wfs,wfc->fsc', source_f[:, 0], receiver_f[:, 1], precision=high)
    imag_real = jnp.einsum('wfs,wfc->fsc', source_f[:, 1], receiver_f[:, 0], precision=high)
    return jnp.stack([real_real + imag_imag, real_imag - imag_real])

def reference(record, valid, sources):
    windows, length, channels = record.shape
    bins = length // 2
    picked = jnp.concatenate([lax.dynamic_slice_in_dim(record, sources[number] * SRC, SRC, 2) for number in range(NBLK)], axis=2)
    picked_flags = jnp.concatenate([lax.dynamic_slice_in_dim(valid, sources[number] * SRC, SRC, 1) for number in range(NBLK)], axis=1)
    source = transform(picked, picked_flags)
    block = math.gcd(channels, 128)
    table = inverse_table(length, bins, LAGS) * (1.0 / math.sqrt(windows * bins))

    def one_block(number):
        start = (number * block).astype(jnp.int32)
        samples = lax.dynamic_slice_in_dim(record, start, block, 2)
        flags = lax.dynamic_slice_in_dim(valid, start, block, 1)
        receiver = transform(samples, flags)
        cross = cross_terms(source, receiver)
        return jnp.einsum('kfl,kfsc->lsc', table, cross, precision=lax.Precision.HIGHEST)
    stacked = lax.map(one_block, jnp.arange(channels // block, dtype=jnp.int32))
    return jnp.transpose(stacked, (1, 2, 0, 3)).reshape(LAGS, NSRC, channels)
```

```python
import functools
import math

import jax
import jax.numpy as jnp
import numpy as np
from jax import lax
from jax.experimental import pallas as pl
from jax.experimental.pallas import tpu as pltpu
from jax.sharding import PartitionSpec as P

SRC = 64
LAGS = 128
HALF_SMOOTH = 5
EPSILON = 1e-05
LEVEL_SHARE = 0.2

VMEM_LIMIT = 56 * 1024 * 1024
TILE_LAGS = 2


def forward_table(length, bins):
    phase = 2.0 * math.pi / length * np.mod(np.outer(np.arange(1, bins + 1), np.arange(length)), length)
    return jnp.asarray(np.concatenate([np.cos(phase), -np.sin(phase)], axis=0), jnp.bfloat16)


def hann_window(length):
    return jnp.asarray(0.5 - 0.5 * np.cos(2.0 * math.pi / length * np.arange(length)), jnp.float32)[:, None]


def band_matrix(bins):
    rows = np.arange(bins)
    near = (np.abs(rows[:, None] - rows[None, :]) <= HALF_SMOOTH).astype(np.float32)
    return jnp.asarray(near, jnp.bfloat16), jnp.asarray(1.0 / near.sum(axis=1, keepdims=True), jnp.float32)


def rotation_tables(length, bins, total_windows):
    shifts = np.arange(LAGS) - LAGS // 2
    phase = 2.0 * math.pi / length * np.mod(np.outer(shifts, np.arange(1, bins + 1)), length)
    scale = 1.0 / math.sqrt(total_windows * bins)
    cos, sin = np.cos(phase) * scale, np.sin(phase) * scale
    return jnp.asarray(np.stack([np.concatenate([cos, cos], 1), np.concatenate([sin, sin], 1)], 1), jnp.float32)


def whiten_kernel(record_ref, valid_ref, table_ref, taper_ref, band_ref, inverse_count_ref, out_ref):
    bins = band_ref.shape[0]
    samples = record_ref[...].astype(jnp.float32)
    centered = samples - jnp.mean(samples, axis=0, keepdims=True)
    tapered = (centered * taper_ref[...]).astype(jnp.bfloat16)
    spectrum = jnp.dot(table_ref[...], tapered, preferred_element_type=jnp.float32)
    real, imag = spectrum[:bins], spectrum[bins:]
    magnitude = jnp.sqrt(real * real + imag * imag)
    band = band_ref[...]
    smooth = jnp.zeros_like(magnitude)
    rest = magnitude
    for _ in range(3):
        piece = rest.astype(jnp.bfloat16)
        rest = rest - piece.astype(jnp.float32)
        smooth = smooth + jnp.dot(band, piece, preferred_element_type=jnp.float32)
    smooth = smooth * inverse_count_ref[...]
    level = jnp.mean(magnitude, axis=0, keepdims=True)
    gain = valid_ref[...].astype(jnp.float32) / (smooth + (LEVEL_SHARE * level + EPSILON))
    out_ref[:bins] = (real * gain).astype(jnp.bfloat16)
    out_ref[bins:] = (imag * gain).astype(jnp.bfloat16)


def whiten(record, valid, wide_count):
    length, channels = record.shape
    bins = length // 2
    shard = channels // wide_count
    tile = min(512, shard)
    per = shard // tile
    band, inverse_count = band_matrix(bins)
    fixed = lambda i: (0, 0)
    return pl.pallas_call(
        whiten_kernel,
        grid=(channels // tile,),
        in_specs=[
            pl.BlockSpec((length, tile), lambda i: (0, i)),
            pl.BlockSpec((1, tile), lambda i: (0, i)),
            pl.BlockSpec((2 * bins, length), fixed),
            pl.BlockSpec((length, 1), fixed),
            pl.BlockSpec((bins, bins), fixed),
            pl.BlockSpec((bins, 1), fixed),
        ],
        out_specs=pl.BlockSpec((None, 2 * bins, tile), lambda i: (i // per, 0, i % per)),
        out_shape=jax.ShapeDtypeStruct((wide_count, 2 * bins, shard), jnp.bfloat16),
        compiler_params=pltpu.CompilerParams(vmem_limit_bytes=VMEM_LIMIT),
        name="whiten",
    )(record, valid, forward_table(length, bins), hann_window(length), band, inverse_count)


def rotate_split(source_ref, rotation_ref, high_ref, low_ref):
    windows, rows, depth = source_ref.shape
    for window in range(windows):
        source = source_ref[window].astype(jnp.float32)
        real, imag = source[:, : depth // 2], source[:, depth // 2 :]
        turned = jnp.concatenate([imag, -real], axis=1)
        for lag in range(rotation_ref.shape[0]):
            value = source * rotation_ref[lag, 0:1] + turned * rotation_ref[lag, 1:2]
            high = value.astype(jnp.bfloat16)
            at = (slice(lag * rows, (lag + 1) * rows), slice(window * depth, (window + 1) * depth))
            high_ref[at] = high
            low_ref[at] = (value - high.astype(jnp.float32)).astype(jnp.bfloat16)


def stack_kernel(source_ref, rotation_ref, receiver_ref, *rest):
    out_ref, high_ref, low_ref = rest[-3:]
    before_ref = rest[0] if len(rest) == 4 else None
    rotate_split(source_ref, rotation_ref, high_ref, low_ref)
    lags, rows, channels = out_ref.shape
    tile = min(256, channels)

    @pl.loop(0, channels // tile)
    def _(number):
        columns = pl.ds(pl.multiple_of(number * tile, tile), tile)
        receiver = receiver_ref[:, columns]
        total = jnp.dot(high_ref[...], receiver, preferred_element_type=jnp.float32)
        total = total + jnp.dot(low_ref[...], receiver, preferred_element_type=jnp.float32)
        total = total.reshape(lags, rows, tile)
        if before_ref is not None:
            total = total + before_ref[:, :, columns]
        out_ref[:, :, columns] = total


def add_stacks(source, rotation, receiver, before):
    windows, rows, depth = source.shape
    channels = receiver.shape[2]
    lags = rotation.shape[0]
    receiver = receiver.reshape(windows * depth, channels)
    block = pl.BlockSpec((TILE_LAGS, rows, channels), lambda i: (i, 0, 0))
    operands = [source, rotation, receiver]
    in_specs = [
        pl.BlockSpec((windows, rows, depth), lambda i: (0, 0, 0)),
        pl.BlockSpec((TILE_LAGS, 2, depth), lambda i: (i, 0, 0)),
        pl.BlockSpec((windows * depth, channels), lambda i: (0, 0)),
    ]
    if before is not None:
        operands.append(before)
        in_specs.append(block)
    flops = 4 * lags * rows * windows * depth * channels
    return pl.pallas_call(
        stack_kernel,
        grid=(lags // TILE_LAGS,),
        in_specs=in_specs,
        out_specs=block,
        out_shape=jax.ShapeDtypeStruct((lags, rows, channels), jnp.float32),
        scratch_shapes=[pltpu.VMEM((TILE_LAGS * rows, windows * depth), jnp.bfloat16)] * 2,
        input_output_aliases={} if before is None else {3: 0},
        compiler_params=pltpu.CompilerParams(vmem_limit_bytes=VMEM_LIMIT),
        cost_estimate=pl.CostEstimate(flops=flops, bytes_accessed=lags * rows * channels * 8, transcendentals=0),
        name="add_stacks",
    )(*operands)


def on_device(record, valid, sources):
    wide_count = lax.axis_size("wide")
    rep_count = lax.axis_size("rep")
    rep = lax.axis_index("rep")
    _, length, channels = record.shape
    bins = length // 2
    shard = channels // wide_count
    total_windows = wide_count * rep_count
    lags = LAGS // rep_count
    whitened = whiten(record[0], valid, wide_count)
    per_shard = shard // SRC
    picked = []
    for number in range(sources.shape[0]):
        block = sources[number]
        start = (block // per_shard, 0, block % per_shard * SRC)
        picked.append(lax.dynamic_slice(whitened, start, (1, length, SRC))[0])
    own_source = jnp.concatenate(picked, axis=1).T
    source = lax.all_gather(own_source, "rep")
    source = lax.all_gather(source, "wide", axis=1)
    receiver = lax.all_to_all(whitened, "wide", split_axis=0, concat_axis=0, tiled=True)
    rotation = lax.dynamic_slice_in_dim(rotation_tables(length, bins, total_windows), rep * lags, lags, 0)
    ring = [(i, (i + 1) % rep_count) for i in range(rep_count)]
    stacks = None
    for step in range(rep_count):
        later = lax.ppermute(receiver, "rep", ring) if step < rep_count - 1 else None
        owner = lax.rem(rep + rep_count - step, rep_count)
        here = lax.dynamic_index_in_dim(source, owner, 0, keepdims=False)
        for first in range(0, wide_count, 8):
            part = slice(first, min(first + 8, wide_count))
            stacks = add_stacks(here[part], rotation, receiver[part], stacks)
        receiver = later
    return stacks


def solution(mesh):
    return jax.shard_map(
        on_device,
        mesh=mesh,
        in_specs=(P(("wide", "rep"), None, None), P(("wide", "rep"), None), P()),
        out_specs=P("rep", None, "wide"),
        check_vma=False,
    )
```

```python
import functools
import functools
import math

import jax
import jax.numpy as jnp
import numpy as np
from jax import lax
from jax.experimental import pallas as pl
from jax.experimental.pallas import tpu as pltpu
from jax.sharding import PartitionSpec as P

SRC = 64
LAGS = 128
HALF_SMOOTH = 5
EPSILON = 1e-05
LEVEL_SHARE = 0.2

VMEM_LIMIT = 56 * 1024 * 1024
PAIR = 2


def forward_table(length, bins):
    phase = 2.0 * math.pi / length * np.mod(np.outer(np.arange(1, bins + 1), np.arange(length)), length)
    return jnp.asarray(np.concatenate([np.cos(phase), -np.sin(phase)], axis=0), jnp.bfloat16)


def hann_window(length):
    return jnp.asarray(0.5 - 0.5 * np.cos(2.0 * math.pi / length * np.arange(length)), jnp.float32)[:, None]


def band_matrix(bins):
    rows = np.arange(bins)
    near = (np.abs(rows[:, None] - rows[None, :]) <= HALF_SMOOTH).astype(np.float32)
    return jnp.asarray(near, jnp.bfloat16), jnp.asarray(1.0 / near.sum(axis=1, keepdims=True), jnp.float32)


def rotation_tables(length, bins, total_windows):
    shifts = np.arange(LAGS) - LAGS // 2
    phase = 2.0 * math.pi / length * np.mod(np.outer(shifts, np.arange(1, bins + 1)), length)
    scale = 1.0 / math.sqrt(total_windows * bins)
    cos, sin = np.cos(phase) * scale, np.sin(phase) * scale
    return jnp.asarray(np.stack([np.concatenate([cos, cos], 1), np.concatenate([sin, sin], 1)], 1), jnp.float32)


def whiten_kernel(record_ref, valid_ref, table_ref, taper_ref, band_ref, inverse_count_ref, out_ref):
    bins = band_ref.shape[0]
    samples = record_ref[...].astype(jnp.float32)
    centered = samples - jnp.mean(samples, axis=0, keepdims=True)
    tapered = (centered * taper_ref[...]).astype(jnp.bfloat16)
    spectrum = jnp.dot(table_ref[...], tapered, preferred_element_type=jnp.float32)
    real, imag = spectrum[:bins], spectrum[bins:]
    magnitude = jnp.sqrt(real * real + imag * imag)
    band = band_ref[...]
    smooth = jnp.zeros_like(magnitude)
    rest = magnitude
    for _ in range(3):
        piece = rest.astype(jnp.bfloat16)
        rest = rest - piece.astype(jnp.float32)
        smooth = smooth + jnp.dot(band, piece, preferred_element_type=jnp.float32)
    smooth = smooth * inverse_count_ref[...]
    level = jnp.mean(magnitude, axis=0, keepdims=True)
    gain = valid_ref[...].astype(jnp.float32) / (smooth + (LEVEL_SHARE * level + EPSILON))
    out_ref[:bins] = (real * gain).astype(jnp.bfloat16)
    out_ref[bins:] = (imag * gain).astype(jnp.bfloat16)


def whiten(record, valid, wide_count, parts, part):
    length, channels = record.shape
    bins = length // 2
    shard = channels // wide_count
    width = shard // parts
    tile = min(512, width)
    per_shard, per = shard // tile, width // tile
    band, inverse_count = band_matrix(bins)
    fixed = lambda i, j: (0, 0)
    columns = lambda i, j: (0, i * per_shard + part * per + j)
    return pl.pallas_call(
        whiten_kernel,
        grid=(wide_count, per),
        in_specs=[
            pl.BlockSpec((length, tile), columns),
            pl.BlockSpec((1, tile), columns),
            pl.BlockSpec((2 * bins, length), fixed),
            pl.BlockSpec((length, 1), fixed),
            pl.BlockSpec((bins, bins), fixed),
            pl.BlockSpec((bins, 1), fixed),
        ],
        out_specs=pl.BlockSpec((None, 2 * bins, tile), lambda i, j: (i, 0, j)),
        out_shape=jax.ShapeDtypeStruct((wide_count, 2 * bins, width), jnp.bfloat16),
        compiler_params=pltpu.CompilerParams(vmem_limit_bytes=VMEM_LIMIT),
        name="whiten",
    )(record, valid, forward_table(length, bins), hann_window(length), band, inverse_count)


def rotate_split(source_ref, rotation_ref, first_lag, window, split_ref):
    _, rows, depth = source_ref.shape
    source = source_ref[window].astype(jnp.float32)
    turned = jnp.concatenate([source[:, depth // 2 :], -source[:, : depth // 2]], axis=1)
    columns = pl.ds(pl.multiple_of(window * depth, depth), depth)
    for lag in range(PAIR):
        rotation = rotation_ref[first_lag + lag]
        value = source * rotation[0:1] + turned * rotation[1:2]
        high = value.astype(jnp.bfloat16)
        split_ref[lag * rows : (lag + 1) * rows, columns] = high
        low = (value - high.astype(jnp.float32)).astype(jnp.bfloat16)
        split_ref[(PAIR + lag) * rows : (PAIR + lag + 1) * rows, columns] = low


def stack_kernel(fresh, source_ref, rotation_ref, receiver_ref, *rest):
    out_ref, even_ref, odd_ref = rest[-3:]
    before_ref = None if fresh else rest[0]
    step = pl.program_id(0)
    windows = source_ref.shape[0]
    _, rows, channels = out_ref.shape
    total_lags = rotation_ref.shape[0]
    tile = min(256, channels)
    tiles = channels // tile
    share = windows // tiles

    @pl.when(step == 0)
    def _():
        @pl.loop(0, windows)
        def _(window):
            rotate_split(source_ref, rotation_ref, 0, window, even_ref)

    for number, (now_ref, later_ref) in enumerate(((even_ref, odd_ref), (odd_ref, even_ref))):
        next_lag = jnp.minimum((2 * step + number + 1) * PAIR, total_lags - PAIR)
        lags = slice(number * PAIR, (number + 1) * PAIR)

        @pl.loop(0, tiles)
        def _(at):
            for offset in range(share):
                rotate_split(source_ref, rotation_ref, next_lag, at * share + offset, later_ref)
            columns = pl.ds(pl.multiple_of(at * tile, tile), tile)
            both = jnp.dot(now_ref[...], receiver_ref[:, columns], preferred_element_type=jnp.float32)
            total = (both[: PAIR * rows] + both[PAIR * rows :]).reshape(PAIR, rows, tile)
            if before_ref is not None:
                total = total + before_ref[lags, :, columns]
            out_ref[lags, :, columns] = total


def add_stacks(source, rotation, receiver, before, fresh, shard, part):
    windows, rows, depth = source.shape
    channels = receiver.shape[2]
    lags = rotation.shape[0]
    receiver = receiver.reshape(windows * depth, channels)
    block = pl.BlockSpec((2 * PAIR, rows, channels), lambda i: (i, 0, part))
    operands = [source, rotation, receiver]
    in_specs = [
        pl.BlockSpec((windows, rows, depth), lambda i: (0, 0, 0)),
        pl.BlockSpec((lags, 2, depth), lambda i: (0, 0, 0)),
        pl.BlockSpec((windows * depth, channels), lambda i: (0, 0)),
    ]
    if before is not None:
        operands.append(before)
        in_specs.append(pl.BlockSpec(memory_space=pl.ANY) if fresh else block)
    flops = 4 * lags * rows * windows * depth * channels
    return pl.pallas_call(
        functools.partial(stack_kernel, fresh),
        grid=(lags // (2 * PAIR),),
        in_specs=in_specs,
        out_specs=block,
        out_shape=jax.ShapeDtypeStruct((lags, rows, shard), jnp.float32),
        scratch_shapes=[pltpu.VMEM((2 * PAIR * rows, windows * depth), jnp.bfloat16)] * 2,
        input_output_aliases={} if before is None else {3: 0},
        compiler_params=pltpu.CompilerParams(vmem_limit_bytes=VMEM_LIMIT),
        cost_estimate=pl.CostEstimate(flops=flops, bytes_accessed=lags * rows * channels * 8, transcendentals=0),
        name="add_stacks",
    )(*operands)


def pick_sources(whitened, sources):
    length, width = whitened[0].shape[1:]
    per_part = width // SRC
    per_shard = per_part * len(whitened)
    picked = []
    for number in range(sources.shape[0]):
        block = sources[number]
        within = block % per_shard
        start = (block // per_shard, 0, within % per_part * SRC)
        found = [lax.dynamic_slice(one, start, (1, length, SRC))[0] for one in whitened]
        chosen = found[0]
        for part in range(1, len(found)):
            chosen = jnp.where(within // per_part == part, found[part], chosen)
        picked.append(chosen)
    return jnp.concatenate(picked, axis=1).T


def on_device(record, valid, sources):
    wide_count = lax.axis_size("wide")
    rep_count = lax.axis_size("rep")
    rep = lax.axis_index("rep")
    _, length, channels = record.shape
    bins = length // 2
    shard = channels // wide_count
    total_windows = wide_count * rep_count
    lags = LAGS // rep_count
    parts = 2 if shard % 512 == 0 else 1
    whitened = [whiten(record[0], valid, wide_count, parts, part) for part in range(parts)]
    ring = [(i, (i + 1) % rep_count) for i in range(rep_count)]
    pass_on = lambda block: lax.ppermute(block, "rep", ring)
    spread = lambda block: lax.all_to_all(block, "wide", split_axis=0, concat_axis=0, tiled=True)
    source = lax.all_gather(pick_sources(whitened, sources), ("wide", "rep"))
    source = source.reshape(wide_count, rep_count, *source.shape[1:])
    rotation = lax.dynamic_slice_in_dim(rotation_tables(length, bins, total_windows), rep * lags, lags, 0)

    stacks, seen = None, set()

    def add(step, part, receiver):
        nonlocal stacks
        owner = lax.rem(rep + rep_count - step, rep_count)
        here = lax.dynamic_index_in_dim(source, owner, 1, keepdims=False)
        for first in range(0, wide_count, 8):
            chosen = slice(first, min(first + 8, wide_count))
            stacks = add_stacks(here[chosen], rotation, receiver[chosen], stacks, part not in seen, shard, part)
            seen.add(part)

    def after_add(block):
        nonlocal stacks
        block, stacks = lax.optimization_barrier((block, stacks))
        return block

    last = parts - 1
    held = spread(whitened[last])
    waiting = [(0, last, held)]
    if parts == 2:
        travelling = whitened[0]
        for step in range(rep_count):
            if step >= 2:
                add(*waiting.pop(0))
                travelling = after_add(travelling)
            waiting.append((step, 0, spread(travelling)))
            if step < rep_count - 1:
                travelling = pass_on(travelling)
        held, _ = lax.optimization_barrier((held, travelling))
    for step in range(1, rep_count):
        held = pass_on(held)
        if parts == 2 and step < rep_count - 1:
            add(*waiting.pop(0))
            held = after_add(held)
        waiting.append((step, last, held))
    for item in waiting:
        add(*item)
    return stacks


def solution(mesh):
    return jax.shard_map(
        on_device,
        mesh=mesh,
        in_specs=(P(("wide", "rep"), None, None), P(("wide", "rep"), None), P()),
        out_specs=P("rep", None, "wide"),
        check_vma=False,
    )
```
